128 devices in a mesh: grp: 16 (over z, x), col: 8 (over y, core).
Axes of the slice: x: 4, y: 4, z: 4, core: 2. Of those that a mesh axis runs over, the one named last changes fastest.
Arguments:
- tokens: bfloat16 [2048, 6144], P(('grp', 'col')), may hold values from -6 to 6
- routes: int32 [2048, 2], P(('grp', 'col')), may hold values from 0 to 7, all different within a row; in each aligned block of 16 rows (0 to 15, 16 to 31, ...) at most 8 rows name the same one
- route_weights: float32 [2048, 2], P(('grp', 'col')), may hold values from 0.1 to 1
- w_gate: bfloat16 [8, 6144, 8192], P('col', None, 'grp'), may hold values from -0.078125 to 0.078125
- w_up: bfloat16 [8, 6144, 8192], P('col', None, 'grp'), may hold values from -0.078125 to 0.078125
- w_down: bfloat16 [8, 8192, 6144], P('col', 'grp'), may hold values from -0.0625 to 0.0625
Outputs:
- mixed: bfloat16 [2048, 6144], P(('grp', 'col'))
The draws below stay inside these ranges and needn't reach their ends.
Inputs may be any that keep to these rules, and one draw needn't show every extreme that they name: `routes`: the two experts of a token differ. In each device's 16 rows no expert is named more than 8 times, a bound that some block reaches; every expert is named somewhere.
All inputs are finite; a program needn't handle non-finite values.
Results may differ from the reference program's by a relative error of at most 0.02.
Values may be sent and summed in bfloat16 or wider, within the bound.
No kernel may reach another device: no remote copies, remote signals or barrier semaphores. Data moves between devices by JAX's collectives and lax.ppermute only.
A program may use at most 128 MiB of HBM per device.

```python
import math
import jax
import jax.numpy as jnp
import numpy as np
from jax import lax

D = 6144
FF = 8192
TOK_DEV = 16
CAP = 8
EXPERTS = 8
FF_DEV = 512
TOKENS = 2048
N_GRP = 16
DEVICES = 128


def block_scale(key, dims, split, least, high):
    factor_of = 1.0
    for dim, parts in split:
        draws = jax.random.uniform(jax.random.fold_in(jax.random.fold_in(key, 6), dim), (parts,), jnp.float32, least / len(split), high / len(split))
        factor_of = factor_of * jnp.repeat(jnp.exp(draws), dims[dim] // parts).reshape((-1,) + (1,) * (len(dims) - 1 - dim))
    return factor_of


def routed_block(rng, own, number, rows, number_of, top, bound, slope):
    ranking = jax.random.permutation(rng, number_of)
    packed, ordinary = load_shares(number_of, rows * top, bound, slope, True), load_shares(number_of, rows * top, bound, slope, False)
    places = jnp.arange(number_of)

    def named(sizes, rotation):
        used = int((sizes > 0).sum())
        fixed = max(1, used // 4)
        passed = fixed + (places - fixed + rotation * (used - fixed)) % max(1, number_of - fixed)
        return jnp.zeros((number_of,), jnp.int32).at[ranking[jnp.where(places < fixed, places, passed)]].set(jnp.asarray(sizes, jnp.int32))

    sizes = jnp.where(number % 4 == 0, named(packed, number // 4), named(ordinary, number - number // 4 - 1))
    mixed = jax.random.permutation(jax.random.fold_in(own, 3), number_of)
    giver, taker = mixed[0:number_of // 2 * 2:2], mixed[1:number_of // 2 * 2:2]
    room = jnp.minimum(sizes[giver] - 1, bound - sizes[taker]) // 2
    room = jnp.where((giver == ranking[0]) | (taker == ranking[0]) | (sizes[taker] == 0), 0, jnp.maximum(room, 0))
    passed = jax.random.randint(jax.random.fold_in(own, 4), (number_of // 2,), 0, 1 << 20) % (room + 1)
    sizes = sizes.at[giver].add(-passed).at[taker].add(passed)
    labels = jnp.searchsorted(jnp.cumsum(sizes), jnp.arange(rows * top), side="right").astype(jnp.int32)
    table = labels.reshape(top, rows).T
    table = table[jax.random.permutation(jax.random.fold_in(own, 1), rows)]
    rotation = jax.random.randint(jax.random.fold_in(own, 2), (rows, 1), 0, top)
    return jnp.take_along_axis(table, (jnp.arange(top)[None, :] + rotation) % top, axis=1)


def load_shares(count, total, most, skew, full):
    weights = [(1 << 20) // math.isqrt(rank ** skew) + 1 for rank in range(1, count + 1)]
    largest = most if full else min(most, max(-(-total // count), total * weights[0] // sum(weights)))
    least = 1 if total - largest >= count - 1 else 0
    counts, rest = [largest] + [least] * (count - 1), total - largest - least * (count - 1)
    while rest > 0:
        free = [i for i in range(1, count) if counts[i] < largest] or [i for i in range(1, count) if counts[i] < most]
        pool, left = sum([weights[i] for i in free]), rest
        for i in free:
            extra = min(most - counts[i], max(1, left * weights[i] // pool), rest)
            counts[i] = counts[i] + extra
            rest = rest - extra
    return np.array(counts)


def noise(own_key, shape, deviation, bound, shards=(), kind=jnp.bfloat16):
    level = block_scale(own_key, shape, shards, -0.22, 0.18) if shards else 1.0
    result = jax.random.normal(own_key, shape, jnp.float32) * deviation * level
    return jnp.minimum(jnp.maximum(result, -bound), bound).astype(kind)


def setup_inputs(seed: int = 0) -> dict:
    arg_keys = jax.random.split(jax.random.key(seed), 7)
    tokens = noise(arg_keys[0], (TOKENS, D), 1.0, 6.0, ((0, 128),))
    routes_keys = jax.random.split(jax.random.fold_in(arg_keys[1], 1), TOKENS // TOK_DEV)
    routes_turns = jax.random.permutation(jax.random.fold_in(arg_keys[1], 3), TOKENS // TOK_DEV)
    routes = jax.vmap(lambda own, number: routed_block(jax.random.fold_in(arg_keys[1], 2), own, number, TOK_DEV, EXPERTS, 2, CAP, 2))(routes_keys, routes_turns).reshape((TOKENS, 2))
    route_weights = jnp.clip(jnp.exp(math.log(1.0) - 2.3025851 * jax.random.uniform(arg_keys[2], (TOKENS, 2), jnp.float32) ** block_scale(arg_keys[2], (TOKENS, 2), ((0, 128),), -0.2, 0.2)), 0.1, 1.0)
    w_gate = noise(arg_keys[3], (EXPERTS, D, FF), D ** -0.5, 0.078125, ((0, 8), (2, 16)))
    w_up = noise(arg_keys[4], (EXPERTS, D, FF), D ** -0.5, 0.078125, ((0, 8), (2, 16)))
    w_down = noise(arg_keys[5], (EXPERTS, FF, D), FF ** -0.5, 0.0625, ((0, 8), (1, 16)))
    return dict(tokens=tokens, routes=routes, route_weights=route_weights, w_gate=w_gate, w_up=w_up, w_down=w_down)


def reference(tokens, routes, route_weights, w_gate, w_up, w_down):
    pair_count = 2 * TOK_DEV
    pair_ids = routes.reshape(DEVICES, pair_count)
    onehot = (pair_ids[:, :, None] == jnp.arange(EXPERTS, dtype=jnp.int32)[None, None, :]).astype(jnp.int32)
    slots = jnp.sum(onehot * (jnp.cumsum(onehot, axis=1) - 1), axis=-1)
    owner = jnp.arange(DEVICES, dtype=jnp.int32)[:, None]
    place = (owner * CAP + slots).reshape(-1).astype(jnp.int32)
    flat_ids = pair_ids.reshape(-1)
    pair_rows = jnp.repeat(tokens, 2, axis=0)
    flat_weights = route_weights.reshape(-1)
    slot_total = DEVICES * CAP

    def per_expert(carry, expert):
        target = jnp.where(flat_ids == expert, place, slot_total).astype(jnp.int32)
        inbox = jnp.zeros((slot_total, D), jnp.bfloat16).at[target].set(pair_rows, mode="drop")
        gate_act = jnp.dot(inbox, w_gate[expert], preferred_element_type=jnp.float32)
        up_act = jnp.dot(inbox, w_up[expert], preferred_element_type=jnp.float32)
        hidden = (jax.nn.silu(gate_act) * up_act).astype(jnp.bfloat16)
        hidden_blocks = jnp.transpose(hidden.reshape(slot_total, N_GRP, FF_DEV), (1, 0, 2))
        down_blocks = w_down[expert].reshape(N_GRP, FF_DEV, D)

        def add_block(total, pieces):
            term = jnp.dot(pieces[0], pieces[1], preferred_element_type=jnp.float32).astype(jnp.bfloat16)
            term = lax.optimization_barrier(term)
            return total + term.astype(jnp.float32), None

        summed, unused = lax.scan(add_block, jnp.zeros((slot_total, D), jnp.float32), (hidden_blocks, down_blocks))
        expert_out = summed.astype(jnp.bfloat16)
        picked = expert_out[jnp.minimum(target, slot_total - 1)].astype(jnp.float32)
        contrib = jnp.where((flat_ids == expert)[:, None], picked * flat_weights[:, None], 0.0)
        return carry + contrib, None

    pairs_sum, unused = lax.scan(per_expert, jnp.zeros((TOKENS * 2, D), jnp.float32), jnp.arange(EXPERTS, dtype=jnp.int32))
    return jnp.sum(pairs_sum.reshape(TOKENS, 2, D), axis=1).astype(jnp.bfloat16)
```

```python
import functools

import jax
import jax.numpy as jnp
from jax import lax
from jax.experimental import pallas as pl
from jax.experimental.pallas import tpu as pltpu
from jax.sharding import PartitionSpec as P

D = 6144
TOK = 16
FF = 512
PART = D // 3
EXPERTS = 8
EXTRA = 128
AXES = ("grp", "col")
ORDER = ((0, 1, 2), (1, 2, 0), (2, 0, 1))


def flat(z, x, y, c):
    return ((z * 4 + x) * 4 + y) * 2 + c


def shift_pairs(axis, steps):
    pairs = []
    for z in range(4):
        for x in range(4):
            for y in range(4):
                for c in range(2):
                    to = [z, x, y]
                    to[axis] = (to[axis] + (steps if c == 0 else -steps)) % 4
                    pairs.append((flat(z, x, y, c), flat(*to, c)))
    return pairs


def shift(value, axis, steps):
    return lax.ppermute(value, AXES, shift_pairs(axis, steps))


def swap_cores(value):
    return lax.ppermute(value, AXES, [(i, i ^ 1) for i in range(128)])


def pack(tokens, routes, route_weights):
    rows = tokens.astype(jnp.float32)
    top = jnp.max(jnp.abs(rows), axis=1, keepdims=True)
    scale = jnp.ones_like(top)
    power = jnp.zeros_like(top)
    for step in (64, 32, 16, 8, 4, 2, 1):
        fits = top * (2.0**step) < 32768.0
        factor = jnp.where(fits, 2.0**step, 1.0)
        top, scale = top * factor, scale * factor
        power = power + jnp.where(fits, float(step), 0.0)
    ids = jnp.arange(EXPERTS, dtype=jnp.int32)
    weight = jnp.sum(jnp.where(routes[:, :, None] == ids, route_weights[:, :, None], 0.0), axis=1)
    high = weight.astype(jnp.float16)
    low = (weight - high.astype(jnp.float32)).astype(jnp.float16)
    pad = jnp.zeros((TOK, EXTRA - 2 * EXPERTS - 1), jnp.float16)
    return jnp.concatenate([(rows * scale).astype(jnp.float16), high, low, power.astype(jnp.float16), pad], axis=1)


def down_kernel(count, idx_ref, h_ref, own_ref, other_ref, *refs):
    added, outs, rows = refs[: 3 * count], refs[3 * count : 3 * count + 3], refs[-1]
    step = pl.program_id(0)

    @pl.when(step == 0)
    def _():
        for p in range(3):
            for b in range(16):
                rows[p, b * TOK : (b + 1) * TOK, :] = h_ref[idx_ref[p * 16 + b]]

    for p in range(3):

        @pl.when(step // 4 == p)
        def _():
            total = jnp.dot(rows[p, :, :FF], own_ref[...], preferred_element_type=jnp.float32)
            total += jnp.dot(rows[p, :, FF:], other_ref[...], preferred_element_type=jnp.float32)
            for k in range(count):
                total += added[3 * k + p][...].astype(jnp.float32)
            outs[p][...] = total.astype(jnp.bfloat16)


def down(idx, hidden, own, other, added):
    count = len(added)
    tile = PART // 4
    block = [pl.BlockSpec((256, tile), functools.partial(lambda p, j, idx: (0, jnp.clip(j - 4 * p, 0, 3)), p)) for p in range(3)]
    return pl.pallas_call(
        functools.partial(down_kernel, count),
        grid_spec=pltpu.PrefetchScalarGridSpec(
            num_scalar_prefetch=1,
            grid=(12,),
            in_specs=[
                pl.BlockSpec((64, TOK, 2 * FF), lambda j, idx: (0, 0, 0)),
                pl.BlockSpec((FF, tile), lambda j, idx: (0, j)),
                pl.BlockSpec((FF, tile), lambda j, idx: (0, j)),
            ]
            + block * count,
            out_specs=block,
            scratch_shapes=[pltpu.VMEM((3, 256, 2 * FF), jnp.bfloat16)],
        ),
        out_shape=[jax.ShapeDtypeStruct((256, PART), jnp.bfloat16)] * 3,
        compiler_params=pltpu.CompilerParams(vmem_limit_bytes=40 * 2**20),
        cost_estimate=pl.CostEstimate(flops=2 * 256 * 1024 * D, bytes_accessed=16 * 2**20, transcendentals=0),
    )(idx, hidden, own, other, *[piece for pieces in added for piece in pieces])


def reduce_phase(parts, phase):
    size = parts[0].shape[0] // 4
    got = [[], [], []]
    for r in (2, 1, 3):
        for p in range(3):
            got[p].append(shift(parts[p][r * size : (r + 1) * size], ORDER[p][phase], -r))
    return [
        (parts[p][:size].astype(jnp.float32) + sum(g.astype(jnp.float32) for g in got[p])).astype(jnp.bfloat16)
        for p in range(3)
    ]


def body(tokens, routes, route_weights, w_gate, w_up, w_down):
    w_gate, w_up, w_down = w_gate[0], w_up[0], w_down[0]
    gate_other, up_other, down_other = swap_cores(w_gate), swap_cores(w_up), swap_cores(w_down)
    grp, col = lax.axis_index("grp"), lax.axis_index("col")
    place = (grp // 4, grp % 4, col // 2)
    core = col % 2
    packed = lax.all_gather(pack(tokens, routes, route_weights), AXES, axis=0, tiled=True)
    packed = packed.reshape(64, 2, TOK, D + EXTRA)
    mine = lax.dynamic_index_in_dim(packed, core, 1, keepdims=False).reshape(1024, D + EXTRA)
    rows = mine[:, :D].astype(jnp.bfloat16)
    notes = mine[:, D:].astype(jnp.float32)
    scale = jnp.exp2(-notes[:, 2 * EXPERTS : 2 * EXPERTS + 1])

    def hidden_of(gate_w, up_w, expert):
        gate_act = jnp.dot(rows, gate_w, preferred_element_type=jnp.float32) * scale
        up_act = jnp.dot(rows, up_w, preferred_element_type=jnp.float32) * scale
        weight = lax.dynamic_slice_in_dim(notes, expert, 1, 1) + lax.dynamic_slice_in_dim(notes, EXPERTS + expert, 1, 1)
        return (jax.nn.silu(gate_act) * up_act * weight).astype(jnp.bfloat16)

    hidden = jnp.concatenate(
        [hidden_of(w_gate, w_up, col), hidden_of(gate_other, up_other, col + 1 - 2 * core)], axis=1
    ).reshape(64, TOK, 2 * FF)

    direction = 1 - 2 * core
    away = [[(place[a] - direction * r) % 4 for r in range(4)] for a in range(3)]

    def blocks(r):
        out = []
        for first, second, third in ORDER:
            for s in range(4):
                for t in range(4):
                    at = [None] * 3
                    at[first], at[second], at[third] = away[first][r], away[second][s], away[third][t]
                    out.append((at[0] * 4 + at[1]) * 4 + at[2])
        return jnp.stack(out).astype(jnp.int32)

    far = down(blocks(2), hidden, w_down, down_other, [])
    far = [shift(far[p], ORDER[p][0], -1) for p in range(3)]
    back = down(blocks(3), hidden, w_down, down_other, [])
    back = [shift(back[p], ORDER[p][0], 1) for p in range(3)]
    near = down(blocks(1), hidden, w_down, down_other, [far])
    near = [shift(near[p], ORDER[p][0], -1) for p in range(3)]
    own = down(blocks(0), hidden, w_down, down_other, [near, back])
    own = reduce_phase(own, 1)
    own = reduce_phase(own, 2)
    return jnp.concatenate(own, axis=1)


def solution(mesh):
    return jax.shard_map(
        body,
        mesh=mesh,
        in_specs=(
            P(("grp", "col"), None),
            P(("grp", "col"), None),
            P(("grp", "col"), None),
            P("col", None, "grp"),
            P("col", None, "grp"),
            P("col", "grp", None),
        ),
        out_specs=P(("grp", "col"), None),
        check_vma=False,
    )
```

```python
import functools

import jax
import jax.numpy as jnp
from jax import lax
from jax.experimental import pallas as pl
from jax.experimental.pallas import tpu as pltpu
from jax.sharding import PartitionSpec as P

D = 6144
TOK = 16
FF = 512
PART = D // 3
EXPERTS = 8
EXTRA = 128
CAP = 8
KTILE = 1024
SPLIT = 1
AXES = ("grp", "col")
ORDER = ((0, 1, 2), (1, 2, 0), (2, 0, 1))


def flat(z, x, y, c):
    return ((z * 4 + x) * 4 + y) * 2 + c


def shift_pairs(axis, steps):
    pairs = []
    for z in range(4):
        for x in range(4):
            for y in range(4):
                for c in range(2):
                    to = [z, x, y]
                    to[axis] = (to[axis] + (steps if c == 0 else -steps)) % 4
                    pairs.append((flat(z, x, y, c), flat(*to, c)))
    return pairs


def shift(value, axis, steps):
    return lax.ppermute(value, AXES, shift_pairs(axis, steps))


def swap_cores(value):
    return lax.ppermute(value, AXES, [(i, i ^ 1) for i in range(128)])


def pack(tokens, routes, route_weights):
    rows = tokens.astype(jnp.float32)
    top = jnp.max(jnp.abs(rows), axis=1, keepdims=True)
    scale = jnp.ones_like(top)
    power = jnp.zeros_like(top)
    for step in (64, 32, 16, 8, 4, 2, 1):
        fits = top * (2.0**step) < 32768.0
        factor = jnp.where(fits, 2.0**step, 1.0)
        top, scale = top * factor, scale * factor
        power = power + jnp.where(fits, float(step), 0.0)
    ids = jnp.arange(EXPERTS, dtype=jnp.int32)
    weight = jnp.sum(jnp.where(routes[:, :, None] == ids, route_weights[:, :, None], 0.0), axis=1)
    pieces = []
    for _ in range(3):
        piece = weight.astype(jnp.bfloat16).astype(jnp.float32)
        pieces.append(piece.astype(jnp.float16))
        weight = weight - piece
    pad = jnp.zeros((TOK, EXTRA - 3 * EXPERTS - 1), jnp.float16)
    return jnp.concatenate([(rows * scale).astype(jnp.float16), *pieces, power.astype(jnp.float16), pad], axis=1)


def hidden_kernel(where_ref, x_ref, notes_ref, g0_ref, u0_ref, g1_ref, u1_ref, out_ref, picks, noted, gate_sum, up_sum):
    step = pl.program_id(0)

    @pl.when(step == 0)
    def _():
        gate_sum[...] = jnp.zeros_like(gate_sum)
        up_sum[...] = jnp.zeros_like(up_sum)
        before = lax.broadcasted_iota(jnp.int32, (256, 256), 0)
        after = lax.broadcasted_iota(jnp.int32, (256, 256), 1)
        earlier = jnp.where((before // TOK == after // TOK) & (before < after), 1.0, 0.0).astype(jnp.bfloat16)
        lane = lax.broadcasted_iota(jnp.int32, (8, EXTRA), 1)
        slot = lax.broadcasted_iota(jnp.int32, (128, 256), 0)
        token = lax.broadcasted_iota(jnp.int32, (128, 256), 1)
        for g in range(4):
            notes = notes_ref[16 * g : 16 * g + 16].reshape(256, EXTRA)
            for e in range(2):
                column = jnp.where(lane == where_ref[1 + e], 1.0, 0.0).astype(jnp.bfloat16)
                weight = lax.dot_general(column, notes, (((1,), (1,)), ((), ())), preferred_element_type=jnp.float32)
                named = jnp.where(weight > 0, 1.0, 0.0)
                rank = jnp.dot(named.astype(jnp.bfloat16), earlier, preferred_element_type=jnp.float32)
                rank = jnp.where(weight > 0, rank, -1.0)[0:1, :]
                pick = (token // TOK == slot // CAP) & (rank == (slot % CAP).astype(jnp.float32))
                pick = jnp.where(pick, 1.0, 0.0).astype(jnp.bfloat16)
                picks[g, 128 * e : 128 * e + 128] = pick
                noted[e, g] = jnp.dot(pick, notes, preferred_element_type=jnp.float32)

    rows = []
    for g in range(4):
        x = x_ref[16 * g : 16 * g + 16].reshape(256, KTILE)
        rows.append(jnp.dot(picks[g], x, preferred_element_type=jnp.float32).astype(jnp.bfloat16))
    for e, gate_ref, up_ref in ((0, g0_ref, u0_ref), (1, g1_ref, u1_ref)):
        taken = jnp.concatenate([r[128 * e : 128 * e + 128] for r in rows], axis=0)
        gate_sum[e] += jnp.dot(taken, gate_ref[...], preferred_element_type=jnp.float32)
        up_sum[e] += jnp.dot(taken, up_ref[...], preferred_element_type=jnp.float32)

    @pl.when(step == pl.num_programs(0) - 1)
    def _():
        lane = lax.broadcasted_iota(jnp.int32, (128, EXTRA), 1)
        for e in range(2):
            expert = where_ref[1 + e]
            mine = (lane == expert) | (lane == expert + EXPERTS) | (lane == expert + 2 * EXPERTS)
            for g in range(4):
                notes = noted[e, g]
                weight = jnp.sum(jnp.where(mine, notes, 0.0), axis=1, keepdims=True)
                power = jnp.sum(jnp.where(lane == 3 * EXPERTS, notes, 0.0), axis=1, keepdims=True)
                scale = jnp.exp2(-power)
                gate = gate_sum[e, 128 * g : 128 * g + 128] * scale
                up = up_sum[e, 128 * g : 128 * g + 128] * scale
                hidden = (gate / (1.0 + jnp.exp(-gate)) * up * weight).astype(jnp.bfloat16)
                spread = lax.dot_general(
                    picks[g, 128 * e : 128 * e + 128], hidden, (((0,), (0,)), ((), ())), preferred_element_type=jnp.float32
                )
                out_ref[16 * g : 16 * g + 16, :, e * FF : (e + 1) * FF] = spread.astype(jnp.bfloat16).reshape(16, TOK, FF)


def hidden_of(packed, where, gate, up, gate_other, up_other):
    weights = pl.BlockSpec((KTILE, FF), lambda k, where: (k, 0))
    return pl.pallas_call(
        hidden_kernel,
        grid_spec=pltpu.PrefetchScalarGridSpec(
            num_scalar_prefetch=1,
            grid=(D // KTILE,),
            in_specs=[
                pl.BlockSpec((64, TOK, KTILE), lambda k, where: (0, 0, k)),
                pl.BlockSpec((64, TOK, EXTRA), lambda k, where: (0, 0, D // EXTRA)),
                weights,
                weights,
                weights,
                weights,
            ],
            out_specs=pl.BlockSpec((64, TOK, 2 * FF), lambda k, where: (0, 0, 0)),
            scratch_shapes=[
                pltpu.VMEM((4, 256, 256), jnp.bfloat16),
                pltpu.VMEM((2, 4, 128, EXTRA), jnp.float32),
                pltpu.VMEM((2, 512, FF), jnp.float32),
                pltpu.VMEM((2, 512, FF), jnp.float32),
            ],
        ),
        out_shape=jax.ShapeDtypeStruct((64, TOK, 2 * FF), jnp.bfloat16),
        compiler_params=pltpu.CompilerParams(vmem_limit_bytes=58 * 2**20),
        cost_estimate=pl.CostEstimate(flops=16 * 10**9, bytes_accessed=40 * 2**20, transcendentals=2**19),
    )(where, packed, packed, gate, up, gate_other, up_other)


def down_kernel(count, idx_ref, h_ref, own_ref, other_ref, *refs):
    added, outs, rows = refs[: 3 * count], refs[3 * count : 3 * count + 3], refs[-1]
    step = pl.program_id(0)

    @pl.when(step == 0)
    def _():
        for p in range(3):
            for b in range(16):
                rows[p, b * TOK : (b + 1) * TOK, :] = h_ref[idx_ref[p * 16 + b]]

    for p in range(3):

        @pl.when(step // SPLIT == p)
        def _():
            total = jnp.dot(rows[p, :, :FF], own_ref[...], preferred_element_type=jnp.float32)
            total += jnp.dot(rows[p, :, FF:], other_ref[...], preferred_element_type=jnp.float32)
            for k in range(count):
                total += added[3 * k + p][...].astype(jnp.float32)
            outs[p][...] = total.astype(jnp.bfloat16)


def down(idx, hidden, own, other, added):
    count = len(added)
    tile = PART // SPLIT
    block = [pl.BlockSpec((256, tile), functools.partial(lambda p, j, idx: (0, jnp.clip(j - SPLIT * p, 0, SPLIT - 1)), p)) for p in range(3)]
    return pl.pallas_call(
        functools.partial(down_kernel, count),
        grid_spec=pltpu.PrefetchScalarGridSpec(
            num_scalar_prefetch=1,
            grid=(3 * SPLIT,),
            in_specs=[
                pl.BlockSpec((64, TOK, 2 * FF), lambda j, idx: (0, 0, 0)),
                pl.BlockSpec((FF, tile), lambda j, idx: (0, j)),
                pl.BlockSpec((FF, tile), lambda j, idx: (0, j)),
            ]
            + block * count,
            out_specs=block,
            scratch_shapes=[pltpu.VMEM((3, 256, 2 * FF), jnp.bfloat16)],
        ),
        out_shape=[jax.ShapeDtypeStruct((256, PART), jnp.bfloat16)] * 3,
        compiler_params=pltpu.CompilerParams(vmem_limit_bytes=58 * 2**20),
        cost_estimate=pl.CostEstimate(flops=2 * 256 * 1024 * D, bytes_accessed=16 * 2**20, transcendentals=0),
    )(idx, hidden, own, other, *[piece for pieces in added for piece in pieces])


def reduce_phase(parts, phase):
    size = parts[0].shape[0] // 4
    got = [[], [], []]
    for r in (2, 1, 3):
        for p in range(3):
            got[p].append(shift(parts[p][r * size : (r + 1) * size], ORDER[p][phase], -r))
    return [
        (parts[p][:size].astype(jnp.float32) + sum(g.astype(jnp.float32) for g in got[p])).astype(jnp.bfloat16)
        for p in range(3)
    ]


def body(tokens, routes, route_weights, w_gate, w_up, w_down):
    w_gate, w_up, w_down = w_gate[0], w_up[0], w_down[0]
    gate_other, up_other, down_other = swap_cores(w_gate), swap_cores(w_up), swap_cores(w_down)
    grp, col = lax.axis_index("grp"), lax.axis_index("col")
    place = (grp // 4, grp % 4, col // 2)
    core = col % 2
    packed = lax.all_gather(pack(tokens, routes, route_weights), AXES, axis=0, tiled=True)
    packed = packed.reshape(64, 2, TOK, D + EXTRA)
    where = jnp.stack([core, col, col + 1 - 2 * core]).astype(jnp.int32)
    rows = lax.dynamic_index_in_dim(packed, core, 1, keepdims=False).astype(jnp.bfloat16)
    hidden = hidden_of(rows, where, w_gate, w_up, gate_other, up_other)

    direction = 1 - 2 * core
    away = [[(place[a] - direction * r) % 4 for r in range(4)] for a in range(3)]

    def blocks(r):
        out = []
        for first, second, third in ORDER:
            for s in range(4):
                for t in range(4):
                    at = [None] * 3
                    at[first], at[second], at[third] = away[first][r], away[second][s], away[third][t]
                    out.append((at[0] * 4 + at[1]) * 4 + at[2])
        return jnp.stack(out).astype(jnp.int32)

    far = down(blocks(2), hidden, w_down, down_other, [])
    far = [shift(far[p], ORDER[p][0], -1) for p in range(3)]
    back = down(blocks(3), hidden, w_down, down_other, [])
    back = [shift(back[p], ORDER[p][0], 1) for p in range(3)]
    near = down(blocks(1), hidden, w_down, down_other, [far])
    last, near = lax.optimization_barrier((blocks(0), near))
    near = [shift(near[p], ORDER[p][0], -1) for p in range(3)]
    own = down(last, hidden, w_down, down_other, [])
    own = [
        (own[p].astype(jnp.float32) + back[p].astype(jnp.float32) + near[p].astype(jnp.float32)).astype(jnp.bfloat16)
        for p in range(3)
    ]
    own = reduce_phase(own, 1)
    own = reduce_phase(own, 2)
    return jnp.concatenate(own, axis=1)


def solution(mesh):
    return jax.shard_map(
        body,
        mesh=mesh,
        in_specs=(
            P(("grp", "col"), None),
            P(("grp", "col"), None),
            P(("grp", "col"), None),
            P("col", None, "grp"),
            P("col", None, "grp"),
            P("col", "grp", None),
        ),
        out_specs=P(("grp", "col"), None),
        check_vma=False,
    )
```

```python
import jax
import jax.numpy as jnp
from jax import lax
from jax.experimental import pallas as pl
from jax.experimental.pallas import tpu as pltpu
from jax.sharding import PartitionSpec as P

D = 6144
TOK = 16
FF = 512
PART = D // 3
EXPERTS = 8
EXTRA = 128
CAP = 8
KTILE = 1024
SPLIT = 1
HALVES = ((1, 256), (1, 0), (0, 0), (0, 256))
AXES = ("grp", "col")
ORDER = ((0, 1, 2), (1, 2, 0), (2, 0, 1))


def flat(z, x, y, c):
    return ((z * 4 + x) * 4 + y) * 2 + c


def shift_pairs(axis, steps):
    pairs = []
    for z in range(4):
        for x in range(4):
            for y in range(4):
                for c in range(2):
                    to = [z, x, y]
                    to[axis] = (to[axis] + (steps if c == 0 else -steps)) % 4
                    pairs.append((flat(z, x, y, c), flat(*to, c)))
    return pairs


def shift(value, axis, steps):
    return lax.ppermute(value, AXES, shift_pairs(axis, steps))


def swap_cores(value):
    return lax.ppermute(value, AXES, [(i, i ^ 1) for i in range(128)])


def pack(tokens, routes, route_weights):
    rows = tokens.astype(jnp.float32)
    top = jnp.max(jnp.abs(rows), axis=1, keepdims=True)
    scale = jnp.ones_like(top)
    power = jnp.zeros_like(top)
    for step in (64, 32, 16, 8, 4, 2, 1):
        fits = top * (2.0**step) < 32768.0
        factor = jnp.where(fits, 2.0**step, 1.0)
        top, scale = top * factor, scale * factor
        power = power + jnp.where(fits, float(step), 0.0)
    ids = jnp.arange(EXPERTS, dtype=jnp.int32)
    weight = jnp.sum(jnp.where(routes[:, :, None] == ids, route_weights[:, :, None], 0.0), axis=1)
    pieces = []
    for _ in range(3):
        piece = weight.astype(jnp.bfloat16).astype(jnp.float32)
        pieces.append(piece.astype(jnp.float16))
        weight = weight - piece
    pad = jnp.zeros((TOK, EXTRA - 3 * EXPERTS - 1), jnp.float16)
    return jnp.concatenate([(rows * scale).astype(jnp.float16), *pieces, power.astype(jnp.float16), pad], axis=1)


def hidden_kernel(where_ref, x_ref, notes_ref, g0_ref, u0_ref, g1_ref, u1_ref, out_ref, picks, noted, gate_sum, up_sum, hidden_all):
    step = pl.program_id(0)

    @pl.when(step == 0)
    def _():
        gate_sum[...] = jnp.zeros_like(gate_sum)
        up_sum[...] = jnp.zeros_like(up_sum)
        before = lax.broadcasted_iota(jnp.int32, (256, 256), 0)
        after = lax.broadcasted_iota(jnp.int32, (256, 256), 1)
        earlier = jnp.where((before // TOK == after // TOK) & (before < after), 1.0, 0.0).astype(jnp.bfloat16)
        lane = lax.broadcasted_iota(jnp.int32, (8, EXTRA), 1)
        slot = lax.broadcasted_iota(jnp.int32, (128, 256), 0)
        token = lax.broadcasted_iota(jnp.int32, (128, 256), 1)
        for g in range(4):
            notes = notes_ref[16 * g : 16 * g + 16].reshape(256, EXTRA)
            for e in range(2):
                column = jnp.where(lane == where_ref[1 + e], 1.0, 0.0).astype(jnp.bfloat16)
                weight = lax.dot_general(column, notes, (((1,), (1,)), ((), ())), preferred_element_type=jnp.float32)
                named = jnp.where(weight > 0, 1.0, 0.0)
                rank = jnp.dot(named.astype(jnp.bfloat16), earlier, preferred_element_type=jnp.float32)
                rank = jnp.where(weight > 0, rank, -1.0)[0:1, :]
                pick = (token // TOK == slot // CAP) & (rank == (slot % CAP).astype(jnp.float32))
                pick = jnp.where(pick, 1.0, 0.0).astype(jnp.bfloat16)
                picks[g, 128 * e : 128 * e + 128] = pick
                noted[e, g] = jnp.dot(pick, notes, preferred_element_type=jnp.float32)

    rows = []
    for g in range(4):
        x = x_ref[16 * g : 16 * g + 16].reshape(256, KTILE)
        rows.append(jnp.dot(picks[g], x, preferred_element_type=jnp.float32).astype(jnp.bfloat16))
    for e, gate_ref, up_ref in ((0, g0_ref, u0_ref), (1, g1_ref, u1_ref)):
        taken = jnp.concatenate([r[128 * e : 128 * e + 128] for r in rows], axis=0)
        gate_sum[e] += jnp.dot(taken, gate_ref[...], preferred_element_type=jnp.float32)
        up_sum[e] += jnp.dot(taken, up_ref[...], preferred_element_type=jnp.float32)

    @pl.when(step == pl.num_programs(0) - 1)
    def _():
        lane = lax.broadcasted_iota(jnp.int32, (128, EXTRA), 1)
        for e in range(2):
            expert = where_ref[1 + e]
            mine = (lane == expert) | (lane == expert + EXPERTS) | (lane == expert + 2 * EXPERTS)
            for g in range(4):
                notes = noted[e, g]
                weight = jnp.sum(jnp.where(mine, notes, 0.0), axis=1, keepdims=True)
                power = jnp.sum(jnp.where(lane == 3 * EXPERTS, notes, 0.0), axis=1, keepdims=True)
                scale = jnp.exp2(-power)
                gate = gate_sum[e, 128 * g : 128 * g + 128] * scale
                up = up_sum[e, 128 * g : 128 * g + 128] * scale
                hidden = (gate / (1.0 + jnp.exp(-gate)) * up * weight).astype(jnp.bfloat16)
                spread = lax.dot_general(
                    picks[g, 128 * e : 128 * e + 128], hidden, (((0,), (0,)), ((), ())), preferred_element_type=jnp.float32
                )
                hidden_all[16 * g : 16 * g + 16, :, e * FF : (e + 1) * FF] = spread.astype(jnp.bfloat16).reshape(16, TOK, FF)
        direction = 1 - 2 * where_ref[0]
        away = [[(where_ref[3 + a] - direction * r + 4) & 3 for r in range(4)] for a in range(3)]
        for p, order in enumerate(ORDER):
            for r in range(4):
                half, start = HALVES[r]
                for i in range(4):
                    for j in range(4):
                        at = dict(zip(order, (away[order[0]][r], away[order[1]][i], away[order[2]][j])))
                        b = start + (4 * i + j) * TOK
                        out_ref[half, p, b : b + TOK, :] = hidden_all[(at[0] * 4 + at[1]) * 4 + at[2]]


def hidden_of(packed, where, gate, up, gate_other, up_other):
    weights = pl.BlockSpec((KTILE, FF), lambda k, where: (k, 0))
    return pl.pallas_call(
        hidden_kernel,
        grid_spec=pltpu.PrefetchScalarGridSpec(
            num_scalar_prefetch=1,
            grid=(D // KTILE,),
            in_specs=[
                pl.BlockSpec((64, TOK, KTILE), lambda k, where: (0, 0, k)),
                pl.BlockSpec((64, TOK, EXTRA), lambda k, where: (0, 0, D // EXTRA)),
                weights,
                weights,
                weights,
                weights,
            ],
            out_specs=pl.BlockSpec((2, 3, 512, 2 * FF), lambda k, where: (0, 0, 0, 0)),
            scratch_shapes=[
                pltpu.VMEM((4, 256, 256), jnp.bfloat16),
                pltpu.VMEM((2, 4, 128, EXTRA), jnp.float32),
                pltpu.VMEM((2, 512, FF), jnp.float32),
                pltpu.VMEM((2, 512, FF), jnp.float32),
                pltpu.VMEM((64, TOK, 2 * FF), jnp.bfloat16),
            ],
        ),
        out_shape=jax.ShapeDtypeStruct((2, 3, 512, 2 * FF), jnp.bfloat16),
        compiler_params=pltpu.CompilerParams(vmem_limit_bytes=58 * 2**20),
        cost_estimate=pl.CostEstimate(flops=16 * 10**9, bytes_accessed=40 * 2**20, transcendentals=2**19),
    )(where, packed, packed, gate, up, gate_other, up_other)


def down_kernel(h_ref, own_ref, other_ref, *outs):
    step = pl.program_id(0)
    total = jnp.dot(h_ref[:, :FF], own_ref[...], preferred_element_type=jnp.float32)
    total += jnp.dot(h_ref[:, FF:], other_ref[...], preferred_element_type=jnp.float32)
    value = total.astype(jnp.bfloat16)
    for p in range(3):

        @pl.when(step // SPLIT == p)
        def _():
            outs[p][...] = value[:256]
            outs[3 + p][...] = value[256:]


def down(half, hidden, own, other):
    tile = PART // SPLIT
    block = [pl.BlockSpec((256, tile), lambda j, p=p: (0, jnp.clip(j - SPLIT * p, 0, SPLIT - 1))) for p in range(3)]
    out = pl.pallas_call(
        down_kernel,
        grid=(3 * SPLIT,),
        in_specs=[
            pl.BlockSpec((None, None, 512, 2 * FF), lambda j: (half, j // SPLIT, 0, 0)),
            pl.BlockSpec((FF, tile), lambda j: (0, j)),
            pl.BlockSpec((FF, tile), lambda j: (0, j)),
        ],
        out_specs=block * 2,
        out_shape=[jax.ShapeDtypeStruct((256, PART), jnp.bfloat16)] * 6,
        compiler_params=pltpu.CompilerParams(vmem_limit_bytes=58 * 2**20),
        cost_estimate=pl.CostEstimate(flops=2 * 512 * 1024 * D, bytes_accessed=20 * 2**20, transcendentals=0),
    )(hidden, own, other)
    return out[:3], out[3:]


def add(*terms):
    return sum(t.astype(jnp.float32) for t in terms).astype(jnp.bfloat16)


def reduce_phase(parts, phase):
    size = parts[0].shape[0] // 4
    got = [[], [], []]
    for r in (2, 1, 3):
        for p in range(3):
            got[p].append(shift(parts[p][r * size : (r + 1) * size], ORDER[p][phase], -r))
    return [
        (parts[p][:size].astype(jnp.float32) + sum(g.astype(jnp.float32) for g in got[p])).astype(jnp.bfloat16)
        for p in range(3)
    ]


def body(tokens, routes, route_weights, w_gate, w_up, w_down):
    w_gate, w_up, w_down = w_gate[0], w_up[0], w_down[0]
    gate_other, up_other, down_other = swap_cores(w_gate), swap_cores(w_up), swap_cores(w_down)
    grp, col = lax.axis_index("grp"), lax.axis_index("col")
    place = (grp // 4, grp % 4, col // 2)
    core = col % 2
    packed = lax.all_gather(pack(tokens, routes, route_weights), AXES, axis=0, tiled=True)
    packed = packed.reshape(64, 2, TOK, D + EXTRA)
    where = jnp.stack([core, col, col + 1 - 2 * core, *place]).astype(jnp.int32)
    rows = lax.dynamic_index_in_dim(packed, core, 1, keepdims=False).astype(jnp.bfloat16)
    hidden = hidden_of(rows, where, w_gate, w_up, gate_other, up_other)

    far, back = down(0, hidden, w_down, down_other)
    hidden, far, back = lax.optimization_barrier((hidden, far, back))
    far = [shift(far[p], ORDER[p][0], -1) for p in range(3)]
    back = [shift(back[p], ORDER[p][0], 1) for p in range(3)]
    near, own = down(1, hidden, w_down, down_other)
    near = [shift(add(near[p], far[p]), ORDER[p][0], -1) for p in range(3)]
    own = [add(own[p], back[p], near[p]) for p in range(3)]
    own = reduce_phase(own, 1)
    own = reduce_phase(own, 2)
    return jnp.concatenate(own, axis=1)


def solution(mesh):
    return jax.shard_map(
        body,
        mesh=mesh,
        in_specs=(
            P(("grp", "col"), None),
            P(("grp", "col"), None),
            P(("grp", "col"), None),
            P("col", None, "grp"),
            P("col", None, "grp"),
            P("col", "grp", None),
        ),
        out_specs=P(("grp", "col"), None),
        check_vma=False,
    )
```

```python
import functools

import jax
import jax.numpy as jnp
from jax import lax
from jax.experimental import pallas as pl
from jax.experimental.pallas import tpu as pltpu
from jax.sharding import PartitionSpec as P

D = 6144
TOK = 16
FF = 512
PART = D // 3
EXPERTS = 8
EXTRA = 128
CAP = 8
KTILE = 1024
SPLIT = 1
HALVES = ((1, 256), (1, 0), (0, 0), (0, 256))
AXES = ("grp", "col")
ORDER = ((0, 1, 2), (1, 2, 0), (2, 0, 1))


def flat(z, x, y, c):
    return ((z * 4 + x) * 4 + y) * 2 + c


def shift_pairs(axis, steps):
    pairs = []
    for z in range(4):
        for x in range(4):
            for y in range(4):
                for c in range(2):
                    to = [z, x, y]
                    to[axis] = (to[axis] + (steps if c == 0 else -steps)) % 4
                    pairs.append((flat(z, x, y, c), flat(*to, c)))
    return pairs


def shift(value, axis, steps):
    return lax.ppermute(value, AXES, shift_pairs(axis, steps))


def swap_cores(value):
    return lax.ppermute(value, AXES, [(i, i ^ 1) for i in range(128)])


def pack(tokens, routes, route_weights):
    rows = tokens.astype(jnp.float32)
    top = jnp.max(jnp.abs(rows), axis=1, keepdims=True)
    scale = jnp.ones_like(top)
    power = jnp.zeros_like(top)
    for step in (64, 32, 16, 8, 4, 2, 1):
        fits = top * (2.0**step) < 32768.0
        factor = jnp.where(fits, 2.0**step, 1.0)
        top, scale = top * factor, scale * factor
        power = power + jnp.where(fits, float(step), 0.0)
    ids = jnp.arange(EXPERTS, dtype=jnp.int32)
    weight = jnp.sum(jnp.where(routes[:, :, None] == ids, route_weights[:, :, None], 0.0), axis=1)
    pieces = []
    for _ in range(3):
        piece = weight.astype(jnp.bfloat16).astype(jnp.float32)
        pieces.append(piece.astype(jnp.float16))
        weight = weight - piece
    pad = jnp.zeros((TOK, EXTRA - 3 * EXPERTS - 1), jnp.float16)
    return jnp.concatenate([(rows * scale).astype(jnp.float16), *pieces, power.astype(jnp.float16), pad], axis=1)


def hidden_kernel(where_ref, x_ref, notes_ref, g0_ref, u0_ref, g1_ref, u1_ref, out_ref, picks, noted, gate_sum, up_sum):
    step = pl.program_id(0)

    @pl.when(step == 0)
    def _():
        gate_sum[...] = jnp.zeros_like(gate_sum)
        up_sum[...] = jnp.zeros_like(up_sum)
        before = lax.broadcasted_iota(jnp.int32, (256, 256), 0)
        after = lax.broadcasted_iota(jnp.int32, (256, 256), 1)
        earlier = jnp.where((before // TOK == after // TOK) & (before < after), 1.0, 0.0).astype(jnp.bfloat16)
        lane = lax.broadcasted_iota(jnp.int32, (8, EXTRA), 1)
        slot = lax.broadcasted_iota(jnp.int32, (128, 256), 0)
        token = lax.broadcasted_iota(jnp.int32, (128, 256), 1)
        for g in range(4):
            notes = notes_ref[16 * g : 16 * g + 16].reshape(256, EXTRA)
            for e in range(2):
                column = jnp.where(lane == where_ref[1 + e], 1.0, 0.0).astype(jnp.bfloat16)
                weight = lax.dot_general(column, notes, (((1,), (1,)), ((), ())), preferred_element_type=jnp.float32)
                named = jnp.where(weight > 0, 1.0, 0.0)
                rank = jnp.dot(named.astype(jnp.bfloat16), earlier, preferred_element_type=jnp.float32)
                rank = jnp.where(weight > 0, rank, -1.0)[0:1, :]
                pick = (token // TOK == slot // CAP) & (rank == (slot % CAP).astype(jnp.float32))
                pick = jnp.where(pick, 1.0, 0.0).astype(jnp.bfloat16)
                picks[g, 128 * e : 128 * e + 128] = pick
                noted[e, g] = jnp.dot(pick, notes, preferred_element_type=jnp.float32)

    rows = []
    for g in range(4):
        x = x_ref[16 * g : 16 * g + 16].reshape(256, KTILE)
        rows.append(jnp.dot(picks[g], x, preferred_element_type=jnp.float32).astype(jnp.bfloat16))
    for e, gate_ref, up_ref in ((0, g0_ref, u0_ref), (1, g1_ref, u1_ref)):
        taken = jnp.concatenate([r[128 * e : 128 * e + 128] for r in rows], axis=0)
        gate_sum[e] += jnp.dot(taken, gate_ref[...], preferred_element_type=jnp.float32)
        up_sum[e] += jnp.dot(taken, up_ref[...], preferred_element_type=jnp.float32)

    @pl.when(step == pl.num_programs(0) - 1)
    def _():
        lane = lax.broadcasted_iota(jnp.int32, (128, EXTRA), 1)
        for e in range(2):
            expert = where_ref[1 + e]
            mine = (lane == expert) | (lane == expert + EXPERTS) | (lane == expert + 2 * EXPERTS)
            for g in range(4):
                notes = noted[e, g]
                weight = jnp.sum(jnp.where(mine, notes, 0.0), axis=1, keepdims=True)
                power = jnp.sum(jnp.where(lane == 3 * EXPERTS, notes, 0.0), axis=1, keepdims=True)
                scale = jnp.exp2(-power)
                gate = gate_sum[e, 128 * g : 128 * g + 128] * scale
                up = up_sum[e, 128 * g : 128 * g + 128] * scale
                hidden = (gate / (1.0 + jnp.exp(-gate)) * up * weight).astype(jnp.bfloat16)
                spread = lax.dot_general(
                    picks[g, 128 * e : 128 * e + 128], hidden, (((0,), (0,)), ((), ())), preferred_element_type=jnp.float32
                )
                out_ref[16 * g : 16 * g + 16, :, e * FF : (e + 1) * FF] = spread.astype(jnp.bfloat16).reshape(16, TOK, FF)


def hidden_of(packed, where, gate, up, gate_other, up_other):
    weights = pl.BlockSpec((KTILE, FF), lambda k, where: (k, 0))
    return pl.pallas_call(
        hidden_kernel,
        grid_spec=pltpu.PrefetchScalarGridSpec(
            num_scalar_prefetch=1,
            grid=(D // KTILE,),
            in_specs=[
                pl.BlockSpec((64, TOK, KTILE), lambda k, where: (0, 0, k)),
                pl.BlockSpec((64, TOK, EXTRA), lambda k, where: (0, 0, D // EXTRA)),
                weights,
                weights,
                weights,
                weights,
            ],
            out_specs=pl.BlockSpec((64, TOK, 2 * FF), lambda k, where: (0, 0, 0)),
            scratch_shapes=[
                pltpu.VMEM((4, 256, 256), jnp.bfloat16),
                pltpu.VMEM((2, 4, 128, EXTRA), jnp.float32),
                pltpu.VMEM((2, 512, FF), jnp.float32),
                pltpu.VMEM((2, 512, FF), jnp.float32),
            ],
        ),
        out_shape=jax.ShapeDtypeStruct((64, TOK, 2 * FF), jnp.bfloat16),
        compiler_params=pltpu.CompilerParams(vmem_limit_bytes=58 * 2**20),
        cost_estimate=pl.CostEstimate(flops=16 * 10**9, bytes_accessed=40 * 2**20, transcendentals=2**19),
    )(where, packed, packed, gate, up, gate_other, up_other)


def down_kernel(half, where_ref, h_ref, own_ref, other_ref, *refs):
    outs, rows = refs[:6], refs[6]
    step = pl.program_id(0)

    @pl.when(step % SPLIT == 0)
    def _():
        direction = 1 - 2 * where_ref[0]
        away = [[(where_ref[3 + a] - direction * r + 4) & 3 for r in range(4)] for a in range(3)]
        for p, order in enumerate(ORDER):

            @pl.when(step // SPLIT == p)
            def _():
                for r in range(4):
                    if HALVES[r][0] != half:
                        continue
                    for i in range(4):
                        for j in range(4):
                            at = dict(zip(order, (away[order[0]][r], away[order[1]][i], away[order[2]][j])))
                            b = HALVES[r][1] + (4 * i + j) * TOK
                            rows[b : b + TOK, :] = h_ref[(at[0] * 4 + at[1]) * 4 + at[2]]

    total = jnp.dot(rows[:, :FF], own_ref[...], preferred_element_type=jnp.float32)
    total += jnp.dot(rows[:, FF:], other_ref[...], preferred_element_type=jnp.float32)
    value = total.astype(jnp.bfloat16)
    for p in range(3):

        @pl.when(step // SPLIT == p)
        def _():
            outs[p][...] = value[:256]
            outs[3 + p][...] = value[256:]


def down(half, where, hidden, own, other):
    tile = PART // SPLIT
    block = [pl.BlockSpec((256, tile), lambda j, where, p=p: (0, jnp.clip(j - SPLIT * p, 0, SPLIT - 1))) for p in range(3)]
    out = pl.pallas_call(
        functools.partial(down_kernel, half),
        grid_spec=pltpu.PrefetchScalarGridSpec(
            num_scalar_prefetch=1,
            grid=(3 * SPLIT,),
            in_specs=[
                pl.BlockSpec((64, TOK, 2 * FF), lambda j, where: (0, 0, 0)),
                pl.BlockSpec((FF, tile), lambda j, where: (0, j)),
                pl.BlockSpec((FF, tile), lambda j, where: (0, j)),
            ],
            out_specs=block * 2,
            scratch_shapes=[pltpu.VMEM((512, 2 * FF), jnp.bfloat16)],
        ),
        out_shape=[jax.ShapeDtypeStruct((256, PART), jnp.bfloat16)] * 6,
        compiler_params=pltpu.CompilerParams(vmem_limit_bytes=58 * 2**20),
        cost_estimate=pl.CostEstimate(flops=2 * 512 * 1024 * D, bytes_accessed=20 * 2**20, transcendentals=0),
    )(where, hidden, own, other)
    return out[:3], out[3:]


def add(*terms):
    return sum(t.astype(jnp.float32) for t in terms).astype(jnp.bfloat16)


def reduce_phase(parts, phase):
    size = parts[0].shape[0] // 4
    got = [[], [], []]
    for r in (2, 1, 3):
        for p in range(3):
            got[p].append(shift(parts[p][r * size : (r + 1) * size], ORDER[p][phase], -r))
    return [
        (parts[p][:size].astype(jnp.float32) + sum(g.astype(jnp.float32) for g in got[p])).astype(jnp.bfloat16)
        for p in range(3)
    ]


def body(tokens, routes, route_weights, w_gate, w_up, w_down):
    w_gate, w_up, w_down = w_gate[0], w_up[0], w_down[0]
    gate_other, up_other, down_other = swap_cores(w_gate), swap_cores(w_up), swap_cores(w_down)
    grp, col = lax.axis_index("grp"), lax.axis_index("col")
    place = (grp // 4, grp % 4, col // 2)
    core = col % 2
    packed = lax.all_gather(pack(tokens, routes, route_weights), AXES, axis=0, tiled=True)
    packed = packed.reshape(64, 2, TOK, D + EXTRA)
    where = jnp.stack([core, col, col + 1 - 2 * core, *place]).astype(jnp.int32)
    rows = lax.dynamic_index_in_dim(packed, core, 1, keepdims=False).astype(jnp.bfloat16)
    hidden = hidden_of(rows, where, w_gate, w_up, gate_other, up_other)

    far, back = down(0, where, hidden, w_down, down_other)
    hidden, far, back = lax.optimization_barrier((hidden, far, back))
    far = [shift(far[p], ORDER[p][0], -1) for p in range(3)]
    back = [shift(back[p], ORDER[p][0], 1) for p in range(3)]
    near, own = down(1, where, hidden, w_down, down_other)
    near = [shift(add(near[p], far[p]), ORDER[p][0], -1) for p in range(3)]
    own = [add(own[p], back[p], near[p]) for p in range(3)]
    own = reduce_phase(own, 1)
    own = reduce_phase(own, 2)
    return jnp.concatenate(own, axis=1)


def solution(mesh):
    return jax.shard_map(
        body,
        mesh=mesh,
        in_specs=(
            P(("grp", "col"), None),
            P(("grp", "col"), None),
            P(("grp", "col"), None),
            P("col", None, "grp"),
            P("col", None, "grp"),
            P("col", "grp", None),
        ),
        out_specs=P(("grp", "col"), None),
        check_vma=False,
    )
```
